128 devices in a mesh: outer: 16 (over z_lo, y, core), blk: 8 (over x, z_hi).
Axes of the slice: x: 4, y: 4, z: 4 (z_hi: 2, z_lo: 2; z = z_hi * 2 + z_lo), core: 2. Of those that a mesh axis runs over, the one named last changes fastest.
Arguments:
- images: bfloat16 [20480, 1152], P(('outer', 'blk')), may hold values from -0.1796875 to 0.1796875
- texts: bfloat16 [20480, 1152], P(('outer', 'blk')), may hold values from -0.1796875 to 0.1796875
- temp: float32 [1], replicated, may hold values from 2 to 12
- bias: float32 [1], replicated, may hold values from -4 to -1
Outputs:
- grad_images: bfloat16 [20480, 1152], P(('outer', 'blk'))
- grad_texts: bfloat16 [20480, 1152], P(('outer', 'blk'))
The draws below stay inside these ranges and needn't reach their ends.
All inputs are finite; a program needn't handle non-finite values.
Results may differ from the reference program's by a relative error of at most 0.018.
Values may be sent and summed in bfloat16 or wider, within the bound.
No kernel may reach another device: no remote copies, remote signals or barrier semaphores. Data moves between devices by JAX's collectives and lax.ppermute only.
A program may use at most 128 MiB of HBM per device.

```python
import math
import jax
import jax.numpy as jnp
from jax import lax

D = 1152
GROUP = 1280
BATCH = 20480
N_OUTER = 16


def block_levels(stream_key, dims, pieces, low, top_value):
    factor_of, own = 1.0, jax.random.fold_in(stream_key, 6)
    for dim, blocks in pieces:
        steps = jnp.exp(jax.random.uniform(jax.random.fold_in(own, dim), (blocks,), jnp.float32, low / len(pieces), top_value / len(pieces)))
        factor_of = factor_of * jnp.repeat(steps, dims[dim] // blocks).reshape([-1 if axis == dim else 1 for axis in range(len(dims))])
    return factor_of


def noise(rng, shape, spread, limit, shards=(), kind=jnp.bfloat16):
    result = jax.random.normal(rng, shape, jnp.float32) * spread
    if len(shards) > 0:
        result = block_levels(rng, shape, shards, -0.22, 0.18) * result
    return jnp.clip(result, min=-limit, max=limit).astype(kind)


def setup_inputs(seed: int = 0) -> dict:
    keys = jax.random.split(jax.random.key(seed), 5)
    return {
        "images": noise(keys[0], (BATCH, D), 0.03, 0.1796875, ((0, 128),)),
        "texts": noise(keys[1], (BATCH, D), 0.03, 0.1796875, ((0, 128),)),
        "temp": jnp.clip(jnp.exp(jax.random.uniform(keys[2], (1,), jnp.float32, math.log(2.0), math.log(12.0))), 2.0, 12.0),
        "bias": jnp.clip(jax.random.uniform(keys[3], (1,), jnp.float32, -4.0, -1.0), -4.0, -1.0),
    }


def normalize(rows):
    values = rows.astype(jnp.float32)
    length = jnp.sqrt(lax.optimization_barrier(jnp.sum(values * values, axis=-1, keepdims=True)) + 1e-06)
    return (values / length, length)

def reference(images, texts, temp, bias):
    scale = temp[0]
    offset = bias[0]
    ximg, img_len = normalize(images)
    xtxt, txt_len = normalize(texts)
    img_n = ximg.astype(jnp.bfloat16).reshape(N_OUTER, GROUP, D)
    txt_n = xtxt.astype(jnp.bfloat16).reshape(N_OUTER, GROUP, D)
    txt_prev = jnp.roll(txt_n, 1, axis=0)
    ident = jnp.eye(GROUP, dtype=jnp.float32)

    def one_group(blocks):
        left, own, prev = blocks
        sig_own = (jax.nn.sigmoid(scale * jnp.dot(left, own.T, preferred_element_type=jnp.float32) + offset) - ident).astype(jnp.bfloat16)
        sig_prev = jax.nn.sigmoid(scale * jnp.dot(left, prev.T, preferred_element_type=jnp.float32) + offset).astype(jnp.bfloat16)
        dimg = scale * (jnp.dot(sig_own, own, preferred_element_type=jnp.float32) + jnp.dot(sig_prev, prev, preferred_element_type=jnp.float32))
        down = scale * jnp.dot(sig_own.T, left, preferred_element_type=jnp.float32)
        dprev = scale * jnp.dot(sig_prev.T, left, preferred_element_type=jnp.float32)
        return (dimg, down, dprev)
    dimg, down, dprev = lax.map(one_group, (img_n, txt_n, txt_prev))
    dtxt = down + jnp.roll(dprev, -1, axis=0)
    dimg = dimg.reshape(BATCH, D)
    dtxt = dtxt.reshape(BATCH, D)
    grad_images = (dimg - ximg * lax.optimization_barrier(jnp.sum(ximg * dimg, axis=-1, keepdims=True))) / img_len
    grad_texts = (dtxt - xtxt * lax.optimization_barrier(jnp.sum(xtxt * dtxt, axis=-1, keepdims=True))) / txt_len
    return (grad_images.astype(jnp.bfloat16), grad_texts.astype(jnp.bfloat16))
```

```python
import functools

import jax
import jax.numpy as jnp
from jax import lax
from jax.experimental import pallas as pl
from jax.experimental.pallas import tpu as pltpu
from jax.sharding import PartitionSpec as P

VMEM = pltpu.VMEM
LIMIT = 48 * 1024 * 1024
BLK_X = 4
BLK_Z = 2


def shift_prev(value, steps):
    count = lax.axis_size("outer")
    return lax.ppermute(value, "outer", [(s, (s + steps) % count) for s in range(count)])


def shift_x(value, steps):
    pairs = [
        (x * BLK_Z + z, (x + steps) % BLK_X * BLK_Z + z)
        for x in range(BLK_X)
        for z in range(BLK_Z)
    ]
    return lax.ppermute(value, "blk", pairs)


def swap_z(value):
    pairs = [
        (x * BLK_Z + z, x * BLK_Z + (BLK_Z - 1 - z))
        for x in range(BLK_X)
        for z in range(BLK_Z)
    ]
    return lax.ppermute(value, "blk", pairs)


def normalized(ref):
    values = ref[...].astype(jnp.float32)
    length = jnp.sqrt(jnp.sum(values * values, axis=-1, keepdims=True) + 1e-06)
    return (values / length).astype(jnp.bfloat16)


def pairs_kernel(
    temp, bias, x0, x1, x2, x3, t0, t1, p0, p1,
    own_img, img1, img2, img3, own_txt, part_txt, prev_own, prev_part,
    txt, img, sig,
):
    rows = x0.shape[0]
    scale, offset = temp[0], bias[0]
    for place, ref in enumerate((t0, t1, p0, p1)):
        txt[place * rows : (place + 1) * rows, :] = normalized(ref)
    for place, (ref, out) in enumerate(
        ((x0, own_img), (x1, img1), (x2, img2), (x3, img3))
    ):
        mine = slice(place * rows, (place + 1) * rows)
        unit = normalized(ref)
        img[mine, :] = unit
        scores = lax.dot_general(
            unit, txt[...], (((1,), (1,)), ((), ())), preferred_element_type=jnp.float32
        )
        weight = jax.nn.sigmoid(scale * scores + offset)
        if place == 0:
            row = lax.broadcasted_iota(jnp.int32, weight.shape, 0)
            col = lax.broadcasted_iota(jnp.int32, weight.shape, 1)
            weight = weight - (row == col).astype(jnp.float32)
        weight = weight.astype(jnp.bfloat16)
        sig[mine, :] = weight
        total = jnp.dot(weight, txt[...], preferred_element_type=jnp.float32)
        out[...] = (scale * total).astype(out.dtype)
    for place, out in enumerate((own_txt, part_txt, prev_own, prev_part)):
        mine = slice(place * rows, (place + 1) * rows)
        total = lax.dot_general(
            sig[:, mine], img[...], (((0,), (0,)), ((), ())),
            preferred_element_type=jnp.float32,
        )
        out[...] = (scale * total).astype(out.dtype)


def finish_kernel(raw, own, *rest):
    out = rest[-1]
    values = raw[...].astype(jnp.float32)
    length = jnp.sqrt(jnp.sum(values * values, axis=-1, keepdims=True) + 1e-06)
    unit = values / length
    total = own[...]
    for ref in rest[:-1]:
        total = total + ref[...].astype(jnp.float32)
    inner = jnp.sum(unit * total, axis=-1, keepdims=True)
    out[...] = ((total - unit * inner) / length).astype(out.dtype)


def finish(raw, own, *received):
    return pl.pallas_call(
        finish_kernel,
        out_shape=jax.ShapeDtypeStruct(raw.shape, jnp.bfloat16),
        in_specs=[pl.BlockSpec(memory_space=VMEM)] * (2 + len(received)),
        out_specs=pl.BlockSpec(memory_space=VMEM),
        compiler_params=pltpu.CompilerParams(vmem_limit_bytes=LIMIT),
        name="finish",
    )(raw, own, *received)


def local(images, texts, temp, bias):
    shape = images.shape
    rows, width = shape
    txt_part = swap_z(texts)
    img_1 = shift_x(images, 1)
    img_3 = shift_x(images, -1)
    img_2 = shift_x(images, 2)
    prev_own = shift_prev(texts, 1)
    prev_part = shift_prev(txt_part, 1)

    wide = jax.ShapeDtypeStruct(shape, jnp.float32)
    sent = jax.ShapeDtypeStruct(shape, jnp.bfloat16)
    smem = pl.BlockSpec(memory_space=pltpu.SMEM)
    vmem = pl.BlockSpec(memory_space=VMEM)
    d0, d1, d2, d3, e_own, e_part, f_own, f_part = pl.pallas_call(
        pairs_kernel,
        out_shape=[wide, sent, sent, sent, wide, wide, sent, sent],
        in_specs=[smem] * 2 + [vmem] * 8,
        out_specs=[vmem] * 8,
        scratch_shapes=[
            VMEM((4 * rows, width), jnp.bfloat16),
            VMEM((4 * rows, width), jnp.bfloat16),
            VMEM((4 * rows, 4 * rows), jnp.bfloat16),
        ],
        compiler_params=pltpu.CompilerParams(vmem_limit_bytes=LIMIT),
        name="pairs",
    )(temp, bias, images, img_1, img_2, img_3, texts, txt_part, prev_own, prev_part)

    back_part = shift_prev(f_part, -1)
    r1 = shift_x(d1, -1)
    r3 = shift_x(d3, 1)
    r2 = shift_x(d2, 2)
    back_own = shift_prev(f_own, -1)
    to_part = (e_part + back_part.astype(jnp.float32)).astype(jnp.bfloat16)
    from_part = swap_z(to_part)
    grad_images = finish(images, d0, r1, r2, r3)
    grad_texts = finish(texts, e_own, back_own, from_part)
    return (grad_images, grad_texts)


def solution(mesh):
    spec = P(("outer", "blk"), None)
    return jax.shard_map(
        local,
        mesh=mesh,
        in_specs=(spec, spec, P(), P()),
        out_specs=(spec, spec),
        check_vma=False,
    )
```

```python
import jax
import jax.numpy as jnp
from jax import lax
from jax.experimental import pallas as pl
from jax.experimental.pallas import tpu as pltpu
from jax.sharding import PartitionSpec as P

VMEM = pltpu.VMEM
LIMIT = 40 * 1024 * 1024
BLK_X = 4
BLK_Z = 2
BF16 = jnp.bfloat16
F32 = jnp.float32


def shift_prev(value, steps):
    count = lax.axis_size("outer")
    return lax.ppermute(value, "outer", [(s, (s + steps) % count) for s in range(count)])


def shift_x(value, steps):
    pairs = [
        (x * BLK_Z + z, (x + steps) % BLK_X * BLK_Z + z)
        for x in range(BLK_X)
        for z in range(BLK_Z)
    ]
    return lax.ppermute(value, "blk", pairs)


def shift_around(value):
    outer, blk = lax.axis_size("outer"), lax.axis_size("blk")
    pairs = []
    for s in range(outer):
        for b in range(blk):
            x = (b // BLK_Z + 1 - s % 2 * 2) % BLK_X
            pairs.append((s * blk + b, s * blk + x * BLK_Z + b % BLK_Z))
    return lax.ppermute(value, ("outer", "blk"), pairs)


def swap_z(value):
    pairs = [
        (x * BLK_Z + z, x * BLK_Z + (BLK_Z - 1 - z))
        for x in range(BLK_X)
        for z in range(BLK_Z)
    ]
    return lax.ppermute(value, "blk", pairs)


def call(body, name, outs, flops, operands, scratch=(), smem=0, aliases=None):
    specs = [pl.BlockSpec(memory_space=pltpu.SMEM)] * smem
    specs += [pl.BlockSpec(memory_space=VMEM)] * (len(operands) - smem)
    size = sum(v.size * v.dtype.itemsize for v in operands)
    return pl.pallas_call(
        body,
        out_shape=outs,
        in_specs=specs,
        out_specs=[pl.BlockSpec(memory_space=VMEM)] * len(outs),
        scratch_shapes=list(scratch),
        input_output_aliases=aliases or {},
        compiler_params=pltpu.CompilerParams(vmem_limit_bytes=LIMIT),
        cost_estimate=pl.CostEstimate(flops=flops, bytes_accessed=0, transcendentals=0),
        name=name,
    )(*operands)


def normalized(ref):
    values = ref[...].astype(F32)
    length = jnp.sqrt(jnp.sum(values * values, axis=-1, keepdims=True) + 1e-06)
    return (values / length).astype(BF16)


def scores(left, right):
    return lax.dot_general(left, right, (((1,), (1,)), ((), ())), preferred_element_type=F32)


def sums(left, right):
    return lax.dot_general(left, right, (((0,), (0,)), ((), ())), preferred_element_type=F32)


def near_units_kernel(core, temp, bias, x1_raw, x3_raw, pair, sent):
    rows = sent.shape[0]
    pair[:rows, :] = normalized(x1_raw)
    pair[rows:, :] = normalized(x3_raw)

    @pl.when(core[0] == 0)
    def _():
        sent[...] = pair[:rows, :]

    @pl.when(core[0] != 0)
    def _():
        sent[...] = pair[rows:, :]


def early_kernel(temp, bias, images, texts, part_raw, p0_raw, pair, img, txt, sig):
    rows = images.shape[0]
    img[:rows, :] = normalized(images)
    img[rows : 3 * rows, :] = pair[...]
    for k, raw in enumerate((texts, part_raw, p0_raw)):
        txt[k * rows : (k + 1) * rows, :] = normalized(raw)
    early = 3 * rows
    value = jax.nn.sigmoid(temp[0] * scores(img[:early, :], txt[:early, :]) + bias[0])
    row = lax.broadcasted_iota(jnp.int32, value.shape, 0)
    col = lax.broadcasted_iota(jnp.int32, value.shape, 1)
    same = jnp.logical_and(row == col, row < rows)
    sig[:early, :early] = (value - same.astype(F32)).astype(BF16)


def late_kernel(
    temp, bias, p1_raw, x2, img_in, txt_in, sig_in, img, txt, sig, d1, d3, d2
):
    rows = p1_raw.shape[0]
    early = 3 * rows
    txt[early:, :] = normalized(p1_raw)
    img[early:, :] = x2[...]
    value = jax.nn.sigmoid(temp[0] * scores(img[early:, :], txt[...]) + bias[0])
    sig[early:, :] = value.astype(BF16)
    value = jax.nn.sigmoid(temp[0] * scores(img[:early, :], txt[early:, :]) + bias[0])
    sig[:early, early:] = value.astype(BF16)
    for k, out in ((1, d1), (2, d3), (3, d2)):
        weight = sig[k * rows : (k + 1) * rows, :]
        total = jnp.dot(weight, txt[...], preferred_element_type=F32)
        out[...] = (temp[0] * total).astype(BF16)


def middle_kernel(
    temp, bias, img, txt, sig, n0_raw, n_pair, d0, e_own, e_part, nxt, sig_next
):
    rows = d0.shape[0]
    early = 3 * rows
    d0[...] = temp[0] * jnp.dot(sig[:rows, :], txt[...], preferred_element_type=F32)
    e_own[...] = temp[0] * sums(sig[:, :rows], img[...])
    e_part[...] = temp[0] * sums(sig[:, rows : 2 * rows], img[...])
    nxt[:rows, :] = normalized(n0_raw)
    nxt[rows:early, :] = n_pair[...]
    value = scores(nxt[:early, :], txt[: 2 * rows, :])
    sig_next[:early, :] = jax.nn.sigmoid(temp[0] * value + bias[0]).astype(BF16)


def part_kernel(temp, bias, n2, txt, e_part, nxt_in, sig_in, nxt, sig_next, to_part):
    rows = n2.shape[0]
    early = 3 * rows
    nxt[early:, :] = n2[...]
    value = scores(nxt[early:, :], txt[: 2 * rows, :])
    sig_next[early:, :] = jax.nn.sigmoid(temp[0] * value + bias[0]).astype(BF16)
    total = e_part[...] + temp[0] * sums(sig_next[:, rows:], nxt[...])
    to_part[...] = total.astype(BF16)


def own_kernel(temp, e_own, nxt, sig_next, out):
    rows = out.shape[0]
    out[...] = e_own[...] + temp[0] * sums(sig_next[:, :rows], nxt[...])


def finish_kernel(raw, own, *rest):
    out = rest[-1]
    values = raw[...].astype(F32)
    length = jnp.sqrt(jnp.sum(values * values, axis=-1, keepdims=True) + 1e-06)
    unit = values / length
    total = own[...]
    for ref in rest[:-1]:
        total = total + ref[...].astype(F32)
    inner = jnp.sum(unit * total, axis=-1, keepdims=True)
    out[...] = ((total - unit * inner) / length).astype(out.dtype)


def local(images, texts, temp, bias):
    shape = images.shape
    rows, width = shape
    many = 4 * rows
    tile = 2 * rows * rows * width
    f32 = jax.ShapeDtypeStruct(shape, F32)
    b16 = jax.ShapeDtypeStruct(shape, BF16)
    stack = jax.ShapeDtypeStruct((many, width), BF16)
    sigs = jax.ShapeDtypeStruct((many, many), BF16)
    halves = jax.ShapeDtypeStruct((many, 2 * rows), BF16)
    wide = jax.ShapeDtypeStruct((2 * rows, width), BF16)
    core = (lax.axis_index("outer") % 2).astype(jnp.int32).reshape(1)

    part_raw = swap_z(texts)
    x1_raw = shift_x(images, 1)
    x3_raw = shift_x(images, -1)
    p0_raw = shift_prev(texts, 1)
    p1_raw = shift_prev(part_raw, 1)
    n0_raw = shift_prev(images, -1)
    pair, sent = call(
        near_units_kernel, "units_near", [wide, b16], 3000000000, (core, temp, bias, x1_raw, x3_raw), smem=3
    )
    x2 = shift_around(sent)
    n_pair = shift_prev(pair, -1)
    n2 = shift_prev(x2, -1)

    img, txt, sig = call(
        early_kernel, "early_pairs", [stack, stack, sigs], 1000000000,
        (temp, bias, images, texts, part_raw, p0_raw, pair), smem=2,
    )
    img, txt, sig, d1, d3, d2 = call(
        late_kernel, "late_pairs", [stack, stack, sigs] + [b16] * 3, 10000000,
        (temp, bias, p1_raw, x2, img, txt, sig), smem=2, aliases={4: 0, 5: 1, 6: 2},
    )
    r1 = shift_x(d1, -1)
    r3 = shift_x(d3, 1)
    r2 = shift_x(d2, 2)
    d0, e_own, e_part, nxt, sig_next = call(
        middle_kernel, "middle_sums", [f32] * 3 + [stack, halves], 0,
        (temp, bias, img, txt, sig, n0_raw, n_pair), smem=2,
    )
    nxt, sig_next, to_part = call(
        part_kernel, "part_sums", [stack, halves, b16], 100000000,
        (temp, bias, n2, txt, e_part, nxt, sig_next), smem=2, aliases={5: 0, 6: 1},
    )
    from_part = swap_z(to_part)
    (e_own,) = call(own_kernel, "own_sums", [f32], 1000000000, (temp, e_own, nxt, sig_next), smem=1)
    (grad_images,) = call(
        finish_kernel, "finish_images", [b16], 100000000000, (images, d0, r1, r3, r2)
    )
    (grad_texts,) = call(
        finish_kernel, "finish_texts", [b16], 100000000, (texts, e_own, from_part)
    )
    return (grad_images, grad_texts)


def solution(mesh):
    spec = P(("outer", "blk"), None)
    return jax.shard_map(
        local,
        mesh=mesh,
        in_specs=(spec, spec, P(), P()),
        out_specs=(spec, spec),
        check_vma=False,
    )
```

```python
import jax
import jax.numpy as jnp
from jax import lax
from jax.experimental import pallas as pl
from jax.experimental.pallas import tpu as pltpu
from jax.sharding import PartitionSpec as P

VMEM = pltpu.VMEM
LIMIT = 40 * 1024 * 1024
BLK_X = 4
BLK_Z = 2
BF16 = jnp.bfloat16
F32 = jnp.float32


def shift_prev(value, steps):
    count = lax.axis_size("outer")
    return lax.ppermute(value, "outer", [(s, (s + steps) % count) for s in range(count)])


def shift_x(value, steps):
    pairs = [
        (x * BLK_Z + z, (x + steps) % BLK_X * BLK_Z + z)
        for x in range(BLK_X)
        for z in range(BLK_Z)
    ]
    return lax.ppermute(value, "blk", pairs)


def shift_around(value, sign):
    outer, blk = lax.axis_size("outer"), lax.axis_size("blk")
    pairs = []
    for s in range(outer):
        for b in range(blk):
            x = (b // BLK_Z + sign * (1 - s % 2 * 2)) % BLK_X
            pairs.append((s * blk + b, s * blk + x * BLK_Z + b % BLK_Z))
    return lax.ppermute(value, ("outer", "blk"), pairs)


def swap_z(value):
    pairs = [
        (x * BLK_Z + z, x * BLK_Z + (BLK_Z - 1 - z))
        for x in range(BLK_X)
        for z in range(BLK_Z)
    ]
    return lax.ppermute(value, "blk", pairs)


def call(body, name, outs, flops, operands, scratch=(), smem=0, aliases=None):
    specs = [pl.BlockSpec(memory_space=pltpu.SMEM)] * smem
    specs += [pl.BlockSpec(memory_space=VMEM)] * (len(operands) - smem)
    size = sum(v.size * v.dtype.itemsize for v in operands)
    return pl.pallas_call(
        body,
        out_shape=outs,
        in_specs=specs,
        out_specs=[pl.BlockSpec(memory_space=VMEM)] * len(outs),
        scratch_shapes=list(scratch),
        input_output_aliases=aliases or {},
        compiler_params=pltpu.CompilerParams(vmem_limit_bytes=LIMIT),
        cost_estimate=pl.CostEstimate(flops=flops, bytes_accessed=0, transcendentals=0),
        name=name,
    )(*operands)


def normalized(ref):
    values = ref[...].astype(F32)
    inverse = 1.0 / jnp.sqrt(jnp.sum(values * values, axis=-1, keepdims=True) + 1e-06)
    return (values * inverse).astype(BF16)


def scores(left, right):
    return lax.dot_general(left, right, (((1,), (1,)), ((), ())), preferred_element_type=F32)


def sums(left, right):
    return lax.dot_general(left, right, (((0,), (0,)), ((), ())), preferred_element_type=F32)


def near_units_kernel(core, temp, bias, x1_raw, x3_raw, pair, sent):
    rows = sent.shape[0]
    pair[:rows, :] = normalized(x1_raw)
    pair[rows:, :] = normalized(x3_raw)

    @pl.when(core[0] == 0)
    def _():
        sent[...] = pair[:rows, :]

    @pl.when(core[0] != 0)
    def _():
        sent[...] = pair[rows:, :]


def unit_kernel(raw, out):
    out[...] = normalized(raw)


def early_kernel(temp, bias, images, texts, part, p0_raw, pair, img, txt, sig):
    rows = images.shape[0]
    img[:rows, :] = normalized(images)
    img[rows : 3 * rows, :] = pair[...]
    txt[:rows, :] = normalized(texts)
    txt[rows : 2 * rows, :] = part[...]
    txt[2 * rows : 3 * rows, :] = normalized(p0_raw)
    early = 3 * rows
    value = jax.nn.sigmoid(temp[0] * scores(img[:early, :], txt[:early, :]) + bias[0])
    row = lax.broadcasted_iota(jnp.int32, value.shape, 0)
    col = lax.broadcasted_iota(jnp.int32, value.shape, 1)
    same = jnp.logical_and(row == col, row < rows)
    sig[:early, :early] = (value - same.astype(F32)).astype(BF16)


def far_kernel(temp, bias, x2, txt, img_in, sig_in, img, sig, acc):
    rows = x2.shape[0]
    early = 3 * rows
    img[early:, :] = x2[...]
    value = jax.nn.sigmoid(temp[0] * scores(x2[...], txt[:early, :]) + bias[0])
    sig[early:, :early] = value.astype(BF16)
    acc[...] = jnp.dot(
        sig[rows:, :early], txt[:early, :], preferred_element_type=F32
    )


def late_kernel(
    temp, bias, p1, acc, img, txt_in, sig_in, txt, sig, d1, d3, d2
):
    rows = p1.shape[0]
    early = 3 * rows
    txt[early:, :] = p1[...]
    value = jax.nn.sigmoid(temp[0] * scores(img[...], p1[...]) + bias[0]).astype(BF16)
    sig[:, early:] = value
    rest = jnp.dot(value[rows:, :], p1[...], preferred_element_type=F32)
    total = temp[0] * (acc[...] + rest)
    for k, out in enumerate((d1, d3, d2)):
        out[...] = total[k * rows : (k + 1) * rows, :].astype(BF16)


def middle_kernel(
    temp, bias, img, txt, sig, n0_raw, n_pair, d0, e_own, e_part, nxt, sig_next
):
    rows = d0.shape[0]
    d0[...] = temp[0] * jnp.dot(sig[:rows, :], txt[...], preferred_element_type=F32)
    nxt[:rows, :] = normalized(n0_raw)
    nxt[rows:, :] = n_pair[...]
    value = scores(nxt[...], txt[: 2 * rows, :])
    sig_next[...] = jax.nn.sigmoid(temp[0] * value + bias[0]).astype(BF16)
    for k, out in enumerate((e_own, e_part)):
        mine = slice(k * rows, (k + 1) * rows)
        out[...] = temp[0] * (sums(sig[:, mine], img[...]) + sums(sig_next[:, mine], nxt[...]))


def part_kernel(temp, bias, n2, txt, e_part, sig_next, to_part):
    rows = n2.shape[0]
    value = scores(n2[...], txt[: 2 * rows, :])
    sig_next[...] = jax.nn.sigmoid(temp[0] * value + bias[0]).astype(BF16)
    total = e_part[...] + temp[0] * sums(sig_next[:, rows:], n2[...])
    to_part[...] = total.astype(BF16)


def own_kernel(temp, e_own, n2, sig_next, out):
    rows = out.shape[0]
    out[...] = e_own[...] + temp[0] * sums(sig_next[:, :rows], n2[...])


def finish_kernel(raw, own, *rest):
    out = rest[-1]
    values = raw[...].astype(F32)
    total = own[...]
    for ref in rest[:-1]:
        total = total + ref[...].astype(F32)
    inverse = 1.0 / jnp.sqrt(jnp.sum(values * values, axis=-1, keepdims=True) + 1e-06)
    inner = jnp.sum(values * total, axis=-1, keepdims=True) * inverse
    out[...] = (total * inverse - values * (inner * inverse * inverse)).astype(out.dtype)


def local(images, texts, temp, bias):
    shape = images.shape
    rows, width = shape
    many = 4 * rows
    tile = 2 * rows * rows * width
    f32 = jax.ShapeDtypeStruct(shape, F32)
    b16 = jax.ShapeDtypeStruct(shape, BF16)
    stack = jax.ShapeDtypeStruct((many, width), BF16)
    sigs = jax.ShapeDtypeStruct((many, many), BF16)
    halves = jax.ShapeDtypeStruct((rows, 2 * rows), BF16)
    wide = jax.ShapeDtypeStruct((2 * rows, width), BF16)
    triple = jax.ShapeDtypeStruct((3 * rows, width), F32)
    core = (lax.axis_index("outer") % 2).astype(jnp.int32).reshape(1)

    part_raw = swap_z(texts)
    x1_raw = shift_x(images, 1)
    x3_raw = shift_x(images, -1)
    later, x1_raw = lax.optimization_barrier((texts, x1_raw))
    p0_raw = shift_prev(later, 1)
    (part,) = call(unit_kernel, "unit_part", [b16], 1000000000, (part_raw,))
    p1 = shift_prev(part, 1)
    later, x3_raw = lax.optimization_barrier((images, x3_raw))
    n0_raw = shift_prev(later, -1)
    pair, sent = call(
        near_units_kernel, "units_near", [wide, b16], 1000000000, (core, temp, bias, x1_raw, x3_raw), smem=3
    )
    x2 = shift_around(sent, 1)
    n_pair = shift_prev(pair, -1)
    n2 = shift_prev(x2, -1)

    img, txt, sig = call(
        early_kernel, "early_pairs", [stack, stack, sigs], 3000000000,
        (temp, bias, images, texts, part, p0_raw, pair), smem=2,
    )
    img, sig, acc = call(
        far_kernel, "far_pairs", [stack, sigs, triple], 1000000000,
        (temp, bias, x2, txt, img, sig), smem=2, aliases={4: 0, 5: 1},
    )
    txt, sig, d1, d3, d2 = call(
        late_kernel, "late_pairs", [stack, sigs] + [b16] * 3, 1000000000,
        (temp, bias, p1, acc, img, txt, sig), smem=2, aliases={5: 0, 6: 1},
    )
    r1 = shift_x(d1, -1)
    r3 = shift_x(d3, 1)
    r2 = shift_x(d2, 2)
    d0, e_own, e_part = call(
        middle_kernel, "middle_sums", [f32] * 3, 1000000000,
        (temp, bias, img, txt, sig, n0_raw, n_pair),
        [VMEM((3 * rows, width), BF16), VMEM((3 * rows, 2 * rows), BF16)], smem=2,
    )
    sig_next, to_part = call(
        part_kernel, "part_sums", [halves, b16], 1000000000,
        (temp, bias, n2, txt, e_part), smem=2,
    )
    from_part = swap_z(to_part)
    (e_own,) = call(own_kernel, "own_sums", [f32], 1000000000, (temp, e_own, n2, sig_next), smem=1)
    (grad_images,) = call(
        finish_kernel, "finish_images", [b16], 1000000000, (images, d0, r1, r3, r2)
    )
    (grad_texts,) = call(
        finish_kernel, "finish_texts", [b16], 1000000000, (texts, e_own, from_part)
    )
    return (grad_images, grad_texts)


def solution(mesh):
    spec = P(("outer", "blk"), None)
    return jax.shard_map(
        local,
        mesh=mesh,
        in_specs=(spec, spec, P(), P()),
        out_specs=(spec, spec),
        check_vma=False,
    )
```

```python
import jax
import jax.numpy as jnp
from jax import lax
from jax.experimental import pallas as pl
from jax.experimental.pallas import tpu as pltpu
from jax.sharding import PartitionSpec as P

VMEM = pltpu.VMEM
LIMIT = 40 * 1024 * 1024
BLK_X = 4
BLK_Z = 2
CHUNKS = 5
BF16 = jnp.bfloat16
F32 = jnp.float32


def shift_prev(value, steps):
    count = lax.axis_size("outer")
    return lax.ppermute(value, "outer", [(s, (s + steps) % count) for s in range(count)])


def shift_x(value, steps):
    pairs = [
        (x * BLK_Z + z, (x + steps) % BLK_X * BLK_Z + z)
        for x in range(BLK_X)
        for z in range(BLK_Z)
    ]
    return lax.ppermute(value, "blk", pairs)


def shift_around(value, sign):
    outer, blk = lax.axis_size("outer"), lax.axis_size("blk")
    pairs = []
    for s in range(outer):
        for b in range(blk):
            x = (b // BLK_Z + sign * (1 - s % 2 * 2)) % BLK_X
            pairs.append((s * blk + b, s * blk + x * BLK_Z + b % BLK_Z))
    return lax.ppermute(value, ("outer", "blk"), pairs)


def swap_z(value):
    pairs = [
        (x * BLK_Z + z, x * BLK_Z + (BLK_Z - 1 - z))
        for x in range(BLK_X)
        for z in range(BLK_Z)
    ]
    return lax.ppermute(value, "blk", pairs)


def call(body, name, outs, flops, operands, scratch=(), smem=0, aliases=None):
    specs = [pl.BlockSpec(memory_space=pltpu.SMEM)] * smem
    specs += [pl.BlockSpec(memory_space=VMEM)] * (len(operands) - smem)
    return pl.pallas_call(
        body,
        out_shape=outs,
        in_specs=specs,
        out_specs=[pl.BlockSpec(memory_space=VMEM)] * len(outs),
        scratch_shapes=list(scratch),
        input_output_aliases=aliases or {},
        compiler_params=pltpu.CompilerParams(vmem_limit_bytes=LIMIT),
        cost_estimate=pl.CostEstimate(flops=flops, bytes_accessed=0, transcendentals=0),
        name=name,
    )(*operands)


def normalized(ref):
    values = ref[...].astype(F32)
    inverse = 1.0 / jnp.sqrt(jnp.sum(values * values, axis=-1, keepdims=True) + 1e-06)
    return (values * inverse).astype(BF16)


def scores(left, right):
    return lax.dot_general(left, right, (((1,), (1,)), ((), ())), preferred_element_type=F32)


def sums(left, right):
    return lax.dot_general(left, right, (((0,), (0,)), ((), ())), preferred_element_type=F32)


def near_units_kernel(core, temp, bias, x1_raw, x3_raw, pair, sent):
    rows = sent.shape[0]
    pair[:rows, :] = normalized(x1_raw)
    pair[rows:, :] = normalized(x3_raw)

    @pl.when(core[0] == 0)
    def _():
        sent[...] = pair[:rows, :]

    @pl.when(core[0] != 0)
    def _():
        sent[...] = pair[rows:, :]


def unit_kernel(raw, out):
    out[...] = normalized(raw)


def early_kernel(temp, bias, images, texts, part, p0_raw, pair, img, txt, sig):
    rows = images.shape[0]
    img[:rows, :] = normalized(images)
    img[rows : 3 * rows, :] = pair[...]
    txt[:rows, :] = normalized(texts)
    txt[rows : 2 * rows, :] = part[...]
    txt[2 * rows : 3 * rows, :] = normalized(p0_raw)
    early = 3 * rows
    value = jax.nn.sigmoid(temp[0] * scores(img[:early, :], txt[:early, :]) + bias[0])
    row = lax.broadcasted_iota(jnp.int32, value.shape, 0)
    col = lax.broadcasted_iota(jnp.int32, value.shape, 1)
    same = jnp.logical_and(row == col, row < rows)
    sig[:early, :early] = (value - same.astype(F32)).astype(BF16)


def far_kernel(temp, bias, x2, txt, img_in, sig_in, img, sig, acc):
    rows = x2.shape[0]
    early = 3 * rows
    img[early:, :] = x2[...]
    value = jax.nn.sigmoid(temp[0] * scores(x2[...], txt[:early, :]) + bias[0])
    sig[early:, :early] = value.astype(BF16)
    acc[...] = jnp.dot(
        sig[rows:, :early], txt[:early, :], preferred_element_type=F32
    )


def late_kernel(
    temp, bias, p1, acc, img, txt_in, sig_in, txt, sig, d1, d3, d2
):
    rows = p1.shape[0]
    early = 3 * rows
    txt[early:, :] = p1[...]
    value = jax.nn.sigmoid(temp[0] * scores(img[...], p1[...]) + bias[0]).astype(BF16)
    sig[:, early:] = value
    rest = jnp.dot(value[rows:, :], p1[...], preferred_element_type=F32)
    total = temp[0] * (acc[...] + rest)
    for k, out in enumerate((d1, d3, d2)):
        out[...] = total[k * rows : (k + 1) * rows, :].astype(BF16)


def middle_kernel(
    temp, bias, img, txt, sig, n0_raw, n_pair, d0, e_own, e_part, nxt, sig_next
):
    rows = d0.shape[0]
    d0[...] = temp[0] * jnp.dot(sig[:rows, :], txt[...], preferred_element_type=F32)
    nxt[:rows, :] = normalized(n0_raw)
    nxt[rows:, :] = n_pair[...]
    value = scores(nxt[...], txt[: 2 * rows, :])
    sig_next[...] = jax.nn.sigmoid(temp[0] * value + bias[0]).astype(BF16)
    for k, out in enumerate((e_own, e_part)):
        mine = slice(k * rows, (k + 1) * rows)
        out[...] = temp[0] * (sums(sig[:, mine], img[...]) + sums(sig_next[:, mine], nxt[...]))


def part_kernel(temp, bias, n2, txt, e_part, sig_next, to_part):
    rows = n2.shape[0]
    value = scores(n2[...], txt[: 2 * rows, :])
    sig_next[...] = jax.nn.sigmoid(temp[0] * value + bias[0]).astype(BF16)
    total = e_part[...] + temp[0] * sums(sig_next[:, rows:], n2[...])
    to_part[...] = total.astype(BF16)


def own_kernel(temp, e_own, n2, sig_next, out):
    rows = out.shape[0]
    out[...] = e_own[...] + temp[0] * sums(sig_next[:, :rows], n2[...])


def finish_kernel(raw, own, *rest):
    *received, out, buffer, sems = rest
    step = buffer.shape[0] // CHUNKS
    copies = []
    for k in range(CHUNKS):
        mine = slice(k * step, (k + 1) * step)
        values = raw[mine, :].astype(F32)
        total = own[mine, :]
        for ref in received:
            total = total + ref[mine, :].astype(F32)
        square = jnp.sum(values * values, axis=-1, keepdims=True)
        inverse = 1.0 / jnp.sqrt(square + 1e-06)
        inner = jnp.sum(values * total, axis=-1, keepdims=True) * inverse
        grad = total * inverse - values * (inner * inverse * inverse)
        buffer[mine, :] = grad.astype(out.dtype)
        copy = pltpu.make_async_copy(buffer.at[mine, :], out.at[mine, :], sems.at[k])
        copy.start()
        copies.append(copy)
    for copy in copies:
        copy.wait()


def finish(name, flops, operands):
    raw = operands[0]
    return pl.pallas_call(
        finish_kernel,
        out_shape=jax.ShapeDtypeStruct(raw.shape, BF16),
        in_specs=[pl.BlockSpec(memory_space=VMEM)] * len(operands),
        out_specs=pl.BlockSpec(memory_space=pl.ANY),
        scratch_shapes=[VMEM(raw.shape, BF16), pltpu.SemaphoreType.DMA((CHUNKS,))],
        compiler_params=pltpu.CompilerParams(vmem_limit_bytes=LIMIT),
        cost_estimate=pl.CostEstimate(flops=flops, bytes_accessed=0, transcendentals=0),
        name=name,
    )(*operands)


def local(images, texts, temp, bias):
    shape = images.shape
    rows, width = shape
    many = 4 * rows
    tile = 2 * rows * rows * width
    f32 = jax.ShapeDtypeStruct(shape, F32)
    b16 = jax.ShapeDtypeStruct(shape, BF16)
    stack = jax.ShapeDtypeStruct((many, width), BF16)
    sigs = jax.ShapeDtypeStruct((many, many), BF16)
    halves = jax.ShapeDtypeStruct((rows, 2 * rows), BF16)
    wide = jax.ShapeDtypeStruct((2 * rows, width), BF16)
    triple = jax.ShapeDtypeStruct((3 * rows, width), F32)
    core = (lax.axis_index("outer") % 2).astype(jnp.int32).reshape(1)

    part_raw = swap_z(texts)
    x1_raw = shift_x(images, 1)
    x3_raw = shift_x(images, -1)
    later, x1_raw = lax.optimization_barrier((texts, x1_raw))
    p0_raw = shift_prev(later, 1)
    (part,) = call(unit_kernel, "unit_part", [b16], 1000000000, (part_raw,))
    p1 = shift_prev(part, 1)
    later, x3_raw = lax.optimization_barrier((images, x3_raw))
    n0_raw = shift_prev(later, -1)
    pair, sent = call(
        near_units_kernel, "units_near", [wide, b16], 1000000000, (core, temp, bias, x1_raw, x3_raw), smem=3
    )
    x2 = shift_around(sent, 1)
    n_pair = shift_prev(pair, -1)
    n2 = shift_prev(x2, -1)

    img, txt, sig = call(
        early_kernel, "early_pairs", [stack, stack, sigs], 3000000000,
        (temp, bias, images, texts, part, p0_raw, pair), smem=2,
    )
    img, sig, acc = call(
        far_kernel, "far_pairs", [stack, sigs, triple], 1000000000,
        (temp, bias, x2, txt, img, sig), smem=2, aliases={4: 0, 5: 1},
    )
    txt, sig, d1, d3, d2 = call(
        late_kernel, "late_pairs", [stack, sigs] + [b16] * 3, 1000000000,
        (temp, bias, p1, acc, img, txt, sig), smem=2, aliases={5: 0, 6: 1},
    )
    r1 = shift_x(d1, -1)
    r3 = shift_x(d3, 1)
    r2 = shift_x(d2, 2)
    d0, e_own, e_part = call(
        middle_kernel, "middle_sums", [f32] * 3, 1000000000,
        (temp, bias, img, txt, sig, n0_raw, n_pair),
        [VMEM((3 * rows, width), BF16), VMEM((3 * rows, 2 * rows), BF16)], smem=2,
    )
    sig_next, to_part = call(
        part_kernel, "part_sums", [halves, b16], 1000000000,
        (temp, bias, n2, txt, e_part), smem=2,
    )
    from_part = swap_z(to_part)
    (e_own,) = call(own_kernel, "own_sums", [f32], 1000000000, (temp, e_own, n2, sig_next), smem=1)
    grad_images = finish("finish_images", 1000000000, (images, d0, r1, r3, r2))
    grad_texts = finish("finish_texts", 1000000000, (texts, e_own, from_part))
    return (grad_images, grad_texts)


def solution(mesh):
    spec = P(("outer", "blk"), None)
    return jax.shard_map(
        local,
        mesh=mesh,
        in_specs=(spec, spec, P(), P()),
        out_specs=(spec, spec),
        check_vma=False,
    )
```

```python
import jax
import jax.numpy as jnp
from jax import lax
from jax.experimental import pallas as pl
from jax.experimental.pallas import tpu as pltpu
from jax.sharding import PartitionSpec as P

VMEM = pltpu.VMEM
LIMIT = 40 * 1024 * 1024
BLK_X = 4
BLK_Z = 2
CHUNKS = 5
BF16 = jnp.bfloat16
F32 = jnp.float32


def shift_prev(value, steps):
    count = lax.axis_size("outer")
    return lax.ppermute(value, "outer", [(s, (s + steps) % count) for s in range(count)])


def shift_x(value, steps):
    pairs = [
        (x * BLK_Z + z, (x + steps) % BLK_X * BLK_Z + z)
        for x in range(BLK_X)
        for z in range(BLK_Z)
    ]
    return lax.ppermute(value, "blk", pairs)


def shift_around(value, sign):
    outer, blk = lax.axis_size("outer"), lax.axis_size("blk")
    pairs = []
    for s in range(outer):
        for b in range(blk):
            x = (b // BLK_Z + sign * (1 - s % 2 * 2)) % BLK_X
            pairs.append((s * blk + b, s * blk + x * BLK_Z + b % BLK_Z))
    return lax.ppermute(value, ("outer", "blk"), pairs)


def swap_z(value):
    pairs = [
        (x * BLK_Z + z, x * BLK_Z + (BLK_Z - 1 - z))
        for x in range(BLK_X)
        for z in range(BLK_Z)
    ]
    return lax.ppermute(value, "blk", pairs)


def call(body, name, outs, flops, operands, scratch=(), smem=0, aliases=None):
    specs = [pl.BlockSpec(memory_space=pltpu.SMEM)] * smem
    specs += [pl.BlockSpec(memory_space=VMEM)] * (len(operands) - smem)
    return pl.pallas_call(
        body,
        out_shape=outs,
        in_specs=specs,
        out_specs=[pl.BlockSpec(memory_space=VMEM)] * len(outs),
        scratch_shapes=list(scratch),
        input_output_aliases=aliases or {},
        compiler_params=pltpu.CompilerParams(vmem_limit_bytes=LIMIT),
        cost_estimate=pl.CostEstimate(flops=flops, bytes_accessed=0, transcendentals=0),
        name=name,
    )(*operands)


def normalized(ref):
    values = ref[...].astype(F32)
    inverse = 1.0 / jnp.sqrt(jnp.sum(values * values, axis=-1, keepdims=True) + 1e-06)
    return (values * inverse).astype(BF16)


def scores(left, right):
    return lax.dot_general(left, right, (((1,), (1,)), ((), ())), preferred_element_type=F32)


def sums(left, right):
    return lax.dot_general(left, right, (((0,), (0,)), ((), ())), preferred_element_type=F32)


def near_units_kernel(core, temp, bias, x1_raw, x3_raw, pair, sent):
    rows = sent.shape[0]
    pair[:rows, :] = normalized(x1_raw)
    pair[rows:, :] = normalized(x3_raw)

    @pl.when(core[0] == 0)
    def _():
        sent[...] = pair[:rows, :]

    @pl.when(core[0] != 0)
    def _():
        sent[...] = pair[rows:, :]


def unit_kernel(raw, out):
    out[...] = normalized(raw)


def early_kernel(temp, bias, images, texts, part, p0_raw, pair, img, txt, sig):
    rows = images.shape[0]
    img[:rows, :] = normalized(images)
    img[rows : 3 * rows, :] = pair[...]
    txt[:rows, :] = normalized(texts)
    txt[rows : 2 * rows, :] = part[...]
    txt[2 * rows : 3 * rows, :] = normalized(p0_raw)
    early = 3 * rows
    value = jax.nn.sigmoid(temp[0] * scores(img[:early, :], txt[:early, :]) + bias[0])
    row = lax.broadcasted_iota(jnp.int32, value.shape, 0)
    col = lax.broadcasted_iota(jnp.int32, value.shape, 1)
    same = jnp.logical_and(row == col, row < rows)
    sig[:early, :early] = (value - same.astype(F32)).astype(BF16)


def far_kernel(temp, bias, x2, txt, img_in, sig_in, img, sig, acc):
    rows = x2.shape[0]
    early = 3 * rows
    img[early:, :] = x2[...]
    value = jax.nn.sigmoid(temp[0] * scores(x2[...], txt[:early, :]) + bias[0])
    sig[early:, :early] = value.astype(BF16)
    acc[...] = jnp.dot(
        sig[rows:, :early], txt[:early, :], preferred_element_type=F32
    )


def late_kernel(
    temp, bias, p1, acc, img, txt_in, sig_in, txt, sig, d1, d3, d2
):
    rows = p1.shape[0]
    early = 3 * rows
    txt[early:, :] = p1[...]
    value = jax.nn.sigmoid(temp[0] * scores(img[...], p1[...]) + bias[0]).astype(BF16)
    sig[:, early:] = value
    rest = jnp.dot(value[rows:, :], p1[...], preferred_element_type=F32)
    total = temp[0] * (acc[...] + rest)
    for k, out in enumerate((d1, d3, d2)):
        out[...] = total[k * rows : (k + 1) * rows, :].astype(BF16)


def middle_kernel(temp, bias, img, txt, sig, n0_raw, n_pair, e_part, nxt, sig_near):
    rows = n0_raw.shape[0]
    nxt[:rows, :] = normalized(n0_raw)
    nxt[rows:, :] = n_pair[...]
    value = scores(nxt[...], txt[: 2 * rows, :])
    sig_near[...] = jax.nn.sigmoid(temp[0] * value + bias[0]).astype(BF16)
    mine = slice(rows, 2 * rows)
    total = sums(sig[:, mine], img[...]) + sums(sig_near[:, mine], nxt[...])
    e_part[...] = temp[0] * total


def part_kernel(temp, bias, n2, txt, e_part, sig_next, to_part):
    rows = n2.shape[0]
    value = scores(n2[...], txt[: 2 * rows, :])
    sig_next[...] = jax.nn.sigmoid(temp[0] * value + bias[0]).astype(BF16)
    total = e_part[...] + temp[0] * sums(sig_next[:, rows:], n2[...])
    to_part[...] = total.astype(BF16)


def own_kernel(temp, img, txt, sig, nxt, sig_near, n2, sig_next, d0, e_own):
    rows = d0.shape[0]
    d0[...] = temp[0] * jnp.dot(sig[:rows, :], txt[...], preferred_element_type=F32)
    total = sums(sig[:, :rows], img[...]) + sums(sig_near[:, :rows], nxt[...])
    e_own[...] = temp[0] * (total + sums(sig_next[:, :rows], n2[...]))


def finish_kernel(raw, own, *rest):
    *received, out, buffer, sems = rest
    step = buffer.shape[0] // CHUNKS
    copies = []
    for k in range(CHUNKS):
        mine = slice(k * step, (k + 1) * step)
        values = raw[mine, :].astype(F32)
        total = own[mine, :]
        for ref in received:
            total = total + ref[mine, :].astype(F32)
        square = jnp.sum(values * values, axis=-1, keepdims=True)
        inverse = 1.0 / jnp.sqrt(square + 1e-06)
        inner = jnp.sum(values * total, axis=-1, keepdims=True) * inverse
        grad = total * inverse - values * (inner * inverse * inverse)
        buffer[mine, :] = grad.astype(out.dtype)
        copy = pltpu.make_async_copy(buffer.at[mine, :], out.at[mine, :], sems.at[k])
        copy.start()
        copies.append(copy)
    for copy in copies:
        copy.wait()


def finish(name, flops, operands):
    raw = operands[0]
    return pl.pallas_call(
        finish_kernel,
        out_shape=jax.ShapeDtypeStruct(raw.shape, BF16),
        in_specs=[pl.BlockSpec(memory_space=VMEM)] * len(operands),
        out_specs=pl.BlockSpec(memory_space=pl.ANY),
        scratch_shapes=[VMEM(raw.shape, BF16), pltpu.SemaphoreType.DMA((CHUNKS,))],
        compiler_params=pltpu.CompilerParams(vmem_limit_bytes=LIMIT),
        cost_estimate=pl.CostEstimate(flops=flops, bytes_accessed=0, transcendentals=0),
        name=name,
    )(*operands)


def local(images, texts, temp, bias):
    shape = images.shape
    rows, width = shape
    many = 4 * rows
    tile = 2 * rows * rows * width
    f32 = jax.ShapeDtypeStruct(shape, F32)
    b16 = jax.ShapeDtypeStruct(shape, BF16)
    stack = jax.ShapeDtypeStruct((many, width), BF16)
    sigs = jax.ShapeDtypeStruct((many, many), BF16)
    halves = jax.ShapeDtypeStruct((rows, 2 * rows), BF16)
    wide = jax.ShapeDtypeStruct((2 * rows, width), BF16)
    triple = jax.ShapeDtypeStruct((3 * rows, width), F32)
    triple_16 = jax.ShapeDtypeStruct((3 * rows, width), BF16)
    thirds = jax.ShapeDtypeStruct((3 * rows, 2 * rows), BF16)
    core = (lax.axis_index("outer") % 2).astype(jnp.int32).reshape(1)

    part_raw = swap_z(texts)
    x1_raw = shift_x(images, 1)
    x3_raw = shift_x(images, -1)
    later, x1_raw = lax.optimization_barrier((texts, x1_raw))
    p0_raw = shift_prev(later, 1)
    (part,) = call(unit_kernel, "unit_part", [b16], 1000000000, (part_raw,))
    p1 = shift_prev(part, 1)
    later, x3_raw = lax.optimization_barrier((images, x3_raw))
    n0_raw = shift_prev(later, -1)
    pair, sent = call(
        near_units_kernel, "units_near", [wide, b16], 1000000000, (core, temp, bias, x1_raw, x3_raw), smem=3
    )
    x2 = shift_around(sent, 1)
    n_pair = shift_prev(pair, -1)
    n2 = shift_prev(x2, -1)

    img, txt, sig = call(
        early_kernel, "early_pairs", [stack, stack, sigs], 3000000000,
        (temp, bias, images, texts, part, p0_raw, pair), smem=2,
    )
    img, sig, acc = call(
        far_kernel, "far_pairs", [stack, sigs, triple], 1000000000,
        (temp, bias, x2, txt, img, sig), smem=2, aliases={4: 0, 5: 1},
    )
    txt, sig, d1, d3, d2 = call(
        late_kernel, "late_pairs", [stack, sigs] + [b16] * 3, 1000000000,
        (temp, bias, p1, acc, img, txt, sig), smem=2, aliases={5: 0, 6: 1},
    )
    r1 = shift_x(d1, -1)
    r3 = shift_x(d3, 1)
    r2 = shift_x(d2, 2)
    e_part, nxt, sig_near = call(
        middle_kernel, "middle_sums", [f32, triple_16, thirds], 1000000000,
        (temp, bias, img, txt, sig, n0_raw, n_pair), smem=2,
    )
    sig_next, to_part = call(
        part_kernel, "part_sums", [halves, b16], 1000000000,
        (temp, bias, n2, txt, e_part), smem=2,
    )
    from_part = swap_z(to_part)
    d0, e_own = call(
        own_kernel, "own_sums", [f32] * 2, 1000000000,
        (temp, img, txt, sig, nxt, sig_near, n2, sig_next), smem=1,
    )
    grad_images = finish("finish_images", 1000000000, (images, d0, r3, r2, r1))
    grad_texts = finish("finish_texts", 1000000000, (texts, e_own, from_part))
    return (grad_images, grad_texts)


def solution(mesh):
    spec = P(("outer", "blk"), None)
    return jax.shard_map(
        local,
        mesh=mesh,
        in_specs=(spec, spec, P(), P()),
        out_specs=(spec, spec),
        check_vma=False,
    )
```
